256 devices in a mesh: dev: 256 (over x, y, z, core).
Axes of the slice: x: 4, y: 4, z: 8, core: 2. Of those that a mesh axis runs over, the one named last changes fastest.
Arguments:
- features: bfloat16 [262144, 768], P('dev'), may hold values from -6 to 6
- eigvecs: bfloat16 [262144, 64], P('dev'), may hold values from -5 to 5
Outputs:
- updated: float32 [262144, 64], P('dev')
The draws below stay inside these ranges and needn't reach their ends.
All inputs are finite; a program needn't handle non-finite values.
Results may differ from the reference program's by a relative error of at most 0.039.
Values may be sent and summed in bfloat16 or wider, within the bound.
A program may use at most 64 MiB of HBM per device.

```python
import math
import jax
import jax.numpy as jnp
from jax import lax

FEAT = 768
RANK = 64
TILES = 1024
ROUNDS = 3
TOTAL = 262144
N_DEV = 256


def block_scale(own_key, extent, pieces, least, largest):
    gain = 1.0
    for dim, shards_of in pieces:
        heights = jax.random.uniform(jax.random.fold_in(jax.random.fold_in(own_key, 6), dim), (shards_of,), jnp.float32, least / len(pieces), largest / len(pieces))
        gain = gain * jnp.repeat(jnp.exp(heights), extent[dim] // shards_of).reshape((-1,) + (1,) * (len(extent) - 1 - dim))
    return gain


def noise(rng, extent, scale, reach, cuts=(), held_as=jnp.bfloat16):
    array = scale * jax.random.normal(rng, extent, jnp.float32)
    if cuts:
        array = array * block_scale(rng, extent, cuts, -0.22, 0.18)
    return jnp.clip(array, -reach, reach).astype(held_as)


def setup_inputs(seed: int = 0) -> dict:
    arg_keys = jax.random.split(jax.random.key(seed), 3)
    features = noise(arg_keys[0], (TOTAL, FEAT), 1.0, 6.0, ((0, 256),))
    eigvecs = noise(arg_keys[1], (TOTAL, RANK), 1.0, 5.0, ((0, 256),))
    return dict(features=features, eigvecs=eigvecs)


def normalize(features):
    values = features.astype(jnp.float32)
    unit = values * lax.rsqrt(lax.optimization_barrier(jnp.mean(values * values, axis=-1, keepdims=True)) + 1e-06)
    return unit.astype(jnp.bfloat16)

def squares(unit):
    values = unit.astype(jnp.float32)
    return lax.optimization_barrier(jnp.sum(values * values, axis=-1))

def affinity(rows_unit, rows_sq, cols_unit, cols_sq):
    width = rows_unit.shape[1]
    kappa = math.sqrt(2.0 * width)
    inner = lax.dot_general(rows_unit, cols_unit, (((1,), (1,)), ((), ())), preferred_element_type=jnp.float32)
    return jnp.exp(kappa * (inner - 0.5 * (rows_sq[:, None] + cols_sq[None, :])) / width)

def zero_diagonal(kernel):
    size = kernel.shape[0]
    index = lax.broadcasted_iota(jnp.int32, (size, size), 0)
    other = lax.broadcasted_iota(jnp.int32, (size, size), 1)
    return jnp.where(index == other, jnp.zeros_like(kernel), kernel)

def reference(features, eigvecs):
    blocks = N_DEV
    unit = normalize(features).reshape(blocks, TILES, FEAT)
    sqnorm = squares(unit)

    def degree_terms(block):
        own = zero_diagonal(affinity(unit[block], sqnorm[block], unit[block], sqnorm[block]))
        rows = lax.optimization_barrier(jnp.sum(own, axis=1))
        columns = []
        for step in range(1, ROUNDS + 1):
            other = (block + step) % blocks
            kernel = affinity(unit[block], sqnorm[block], unit[other], sqnorm[other])
            rows = rows + lax.optimization_barrier(jnp.sum(kernel, axis=1))
            columns.append(lax.optimization_barrier(jnp.sum(kernel, axis=0)))
        return (rows, jnp.stack(columns))
    rows, columns = lax.map(degree_terms, jnp.arange(blocks, dtype=jnp.int32))
    degree = rows
    for step in range(1, ROUNDS + 1):
        degree = degree + jnp.roll(columns[:, step - 1], step, axis=0)
    inverse = lax.rsqrt(degree)
    scaled = (eigvecs.astype(jnp.float32).reshape(blocks, TILES, RANK) * inverse[:, :, None]).astype(jnp.bfloat16)

    def product_terms(block):
        own = zero_diagonal(affinity(unit[block], sqnorm[block], unit[block], sqnorm[block])).astype(jnp.bfloat16)
        total = jnp.dot(own, scaled[block], preferred_element_type=jnp.float32)
        backs = []
        for step in range(1, ROUNDS + 1):
            other = (block + step) % blocks
            kernel = affinity(unit[block], sqnorm[block], unit[other], sqnorm[other]).astype(jnp.bfloat16)
            total = total + jnp.dot(kernel, scaled[other], preferred_element_type=jnp.float32)
            backs.append(lax.dot_general(kernel, scaled[block], (((0,), (0,)), ((), ())), preferred_element_type=jnp.float32))
        return (total, jnp.stack(backs))
    totals, backs = lax.map(product_terms, jnp.arange(blocks, dtype=jnp.int32))
    for step in range(1, ROUNDS + 1):
        totals = totals + jnp.roll(backs[:, step - 1], step, axis=0)
    factor = 0.25 * math.sqrt((2 * ROUNDS + 1) * TILES)
    updated = factor * inverse[:, :, None] * totals
    return updated.reshape(TOTAL, RANK)
```

```python
import functools
import math

import jax
import jax.numpy as jnp
from jax import lax
from jax.experimental import pallas as pl
from jax.experimental.pallas import tpu as pltpu
from jax.sharding import PartitionSpec as P

ROUNDS = 3
MESH = pl.DeviceIdType.MESH
OWN, SIB, F1, F2, G = range(5)
CR = 256
RELAY = False
F32, BF16 = jnp.float32, jnp.bfloat16


def upward(chip):
    if not RELAY:
        return chip >= 0
    return chip // 32 < 2


class Place:
    def __init__(self, dev, count):
        wrap = lambda i: lax.rem(i + 2 * count, count)
        self.dev, self.count = dev, count
        self.core = lax.rem(dev, 2)
        chip = dev // 2
        s = 2 * self.core - 1
        self.ahead = wrap(dev + 2 * s)
        self.behind = wrap(dev - 2 * s)
        self.far = wrap(dev - 3 * s)
        self.sib = dev - s
        self.side = wrap(dev + s)
        before = lax.rem(chip + count // 2 - 1, count // 2)
        first = self.core == 0
        self.two = jnp.where(first, jnp.logical_not(upward(chip)), upward(before))
        other = jnp.where(first, upward(before), jnp.logical_not(upward(chip)))
        self.cross = jnp.where(self.two == other, self.core == 1, self.two)
        self.one = jnp.logical_not(self.two)
        self.pair = jnp.logical_not(self.cross)
        self.uses_sib = jnp.logical_or(self.one, self.pair)
        x = chip // 32
        edge = jnp.logical_and(self.core == 1, lax.rem(chip, 32) == 0)
        flipped = jnp.where(edge, x + 1 - 2 * lax.rem(x, 2), 3 - x)
        self.relay = dev + (flipped - x) * 64
        self.s = s
        self.wrap = wrap


def kernel(count, x_hbm, e_hbm, o_ref, raw, eig, blk, rel, kst, bl, dacc, dmsg, drecv, sbuf, ymsg, yrecv, yacc,
           load_sem, sib_s, sib_r, f1_s, f1_r, f2_s, f2_r, g_s, g_r, rel_s, rel_r, d_s, d_r, v_s, v_r, y_s, y_r):
    tiles, width = raw.shape
    chunks = tiles // CR
    half = chunks // 2 if RELAY else chunks
    a = math.sqrt(2.0 * width) / width * math.log2(math.e)
    me = Place(lax.axis_index("dev"), count)
    sib = Place(me.sib, count)
    side = Place(me.side, count)

    loads = [pltpu.make_async_copy(x_hbm.at[pl.ds(c * CR, CR)], raw.at[pl.ds(c * CR, CR)], load_sem.at[c]) for c in range(chunks)]
    loads.append(pltpu.make_async_copy(e_hbm, eig, load_sem.at[chunks]))
    for load in loads:
        load.start()

    partners = [me.sib, me.ahead, me.behind, me.far, me.side]
    if RELAY:
        relayed = Place(me.relay, count)
        onward = me.wrap(me.relay - 3 * me.s)
        source = Place(me.far, count).relay
        partners += [me.relay, onward, source]
    barrier = pltpu.get_barrier_semaphore()
    for partner in partners:
        pl.semaphore_signal(barrier, inc=1, device_id=(partner,), device_id_type=MESH)

    def rows(c):
        return pl.ds(c * CR if isinstance(c, int) else pl.multiple_of(c * CR, CR), CR)

    def remote(src, dst, send, recv, to):
        return pltpu.make_async_remote_copy(src_ref=src, dst_ref=dst, send_sem=send, recv_sem=recv, device_id=(to,), device_id_type=MESH)

    def to_sib(c):
        return remote(blk.at[OWN, rows(c)], blk.at[SIB, rows(c)], sib_s.at[c], sib_r.at[c], me.sib)

    def to_ahead(c):
        return remote(blk.at[OWN, rows(c)], blk.at[F1, rows(c)], f1_s.at[c], f1_r.at[c], me.ahead)

    def to_far(c):
        return remote(blk.at[OWN, rows(c)], blk.at[F2, rows(c)], f2_s.at[c], f2_r.at[c], me.far)

    def to_relay(c):
        return remote(blk.at[OWN, rows(c)], rel.at[rows(c - half)], rel_s.at[c - half], rel_r.at[c - half], me.relay)

    def to_onward(c):
        return remote(rel.at[rows(c - half)], blk.at[F2, rows(c)], f2_s.at[c], f2_r.at[c], onward)

    def to_g(c):
        return remote(blk.at[F1, rows(c)], blk.at[G, rows(c)], g_s.at[c], g_r.at[c], me.sib)

    eye = lax.broadcasted_iota(jnp.int32, (128, 128), 0) == lax.broadcasted_iota(jnp.int32, (128, 128), 1)

    def laid(column):
        parts = []
        for start in range(0, column.shape[0], 128):
            wide = jnp.broadcast_to(column[start:start + 128], (128, 128))
            parts.append(jnp.sum(jnp.where(eye, wide, 0.0), axis=0, keepdims=True))
        return jnp.concatenate(parts, axis=1)

    def offsets(unit):
        values = unit.astype(F32)
        return (0.5 * a) * jnp.sum(values * values, axis=-1, keepdims=True)

    def normalize(c):
        values = raw[rows(c), :].astype(F32)
        mean = jnp.mean(values * values, axis=-1, keepdims=True)
        unit = (values * lax.rsqrt(mean + 1e-06)).astype(BF16)
        blk[OWN, rows(c), :] = unit
        bl[OWN, :, rows(c)] = laid(offsets(unit))

    def lay_offsets(slot):
        @pl.loop(0, chunks)
        def _(c):
            bl[slot, :, rows(c)] = laid(offsets(blk[slot, rows(c), :]))

    def tile(row_slot, c, col_slot, store, diagonal=False):
        unit = blk[row_slot, rows(c), :]
        inner = lax.dot_general(unit, blk[col_slot], (((1,), (1,)), ((), ())), preferred_element_type=F32)
        value = jnp.exp2(a * inner - offsets(unit) - bl[col_slot])
        if diagonal:
            at = lax.broadcasted_iota(jnp.int32, value.shape, 0) + c * CR
            value = jnp.where(at == lax.broadcasted_iota(jnp.int32, value.shape, 1), 0.0, value)
        kst[store, rows(c), :] = value.astype(BF16)
        dacc[col_slot] += jnp.sum(value, axis=0, keepdims=True)
        if not diagonal:
            dacc[row_slot, :, rows(c)] += laid(jnp.sum(value, axis=1, keepdims=True))

    dacc[...] = jnp.zeros_like(dacc)
    for c in range(chunks):
        loads[c].wait()
        normalize(c)
        if c == 0:
            pl.semaphore_wait(barrier, len(partners))
        to_ahead(c).start()
        if RELAY and c >= half:
            @pl.when(me.one)
            def _():
                to_relay(c).start()
        to_sib(c).start()

    loads[chunks].wait()
    for c in range(tiles // 128):
        part = eig[c * 128:(c + 1) * 128, :].astype(F32)
        yacc[0, :, c * 128:(c + 1) * 128] = part.T

    @pl.loop(0, chunks)
    def _(c):
        tile(OWN, c, OWN, 0, diagonal=True)

    for c in range(chunks):
        to_sib(c).wait_recv()
    lay_offsets(SIB)

    @pl.when(me.pair)
    def _():
        @pl.loop(0, chunks)
        def _(c):
            tile(OWN, c, SIB, 3)

    @pl.loop(0, chunks)
    def _(c):
        to_ahead(c).wait_recv()

        @pl.when(sib.cross)
        def _():
            to_g(c).start()

        @pl.when(c == chunks - 2)
        def _():
            @pl.when(me.one)
            def _():
                @pl.loop(0, half)
                def _(i):
                    to_far(i).start()

            if RELAY:
                @pl.when(relayed.one)
                def _():
                    @pl.loop(half, chunks)
                    def _(i):
                        to_relay(i).wait_recv()
                        to_onward(i).start()

        tile(F1, c, OWN, 1)

        @pl.when(me.one)
        def _():
            tile(F1, c, SIB, 2)

    @pl.when(me.cross)
    def _():
        for c in range(chunks):
            to_g(c).wait_recv()
        lay_offsets(G)

        @pl.loop(0, chunks)
        def _(c):
            tile(F1, c, G, 3)

    @pl.when(me.two)
    def _():
        @pl.loop(0, chunks)
        def _(c):
            to_far(c).wait_recv()
            tile(F2, c, OWN, 2)

    def exchange(src, dst, send, recv, pick):
        holders = (
            (F1, me.behind, None, me.ahead, None),
            (G, me.side, me.cross, me.side, side.cross),
            (F2, me.far, me.two, me.far, me.one),
            (SIB, me.sib, me.uses_sib, me.sib, sib.uses_sib),
        )
        out = {}
        for slot, owner, held, holder, lent in holders:
            if pick == 0:
                out[slot] = (remote(src.at[slot], dst.at[slot], send.at[slot], recv.at[slot], owner), held, lent)
            else:
                out[slot] = (remote(src.at[OWN], dst.at[slot], send.at[slot], recv.at[slot], holder), lent, held)
        return out

    def given(condition, action):
        if condition is None:
            action()
        else:
            pl.when(condition)(action)

    degrees = exchange(dmsg, drecv, d_s, d_r, 0)
    dmsg[...] = dacc[...]
    for slot in (F1, F2, G, SIB):
        copy, sends, _ = degrees[slot]
        given(sends, copy.start)
    for slot in (SIB, G, F2, F1):
        copy, _, receives = degrees[slot]

        def add(copy=copy, slot=slot):
            copy.wait_recv()
            dacc[OWN] += drecv[slot]

        given(receives, add)
    inverse = lax.rsqrt(dacc[OWN])
    sbuf[OWN] = (yacc[0] * inverse).astype(BF16)

    scaled = exchange(sbuf, sbuf, v_s, v_r, 1)
    for slot in (G, F1, F2, SIB):
        copy, sends, _ = scaled[slot]
        given(sends, copy.start)

    def by_columns(slot, store):
        return jnp.dot(sbuf[slot], kst[store], preferred_element_type=F32)

    def by_rows(slot, store):
        return lax.dot_general(sbuf[slot], kst[store], (((1,), (1,)), ((), ())), preferred_element_type=F32)

    returned = exchange(ymsg, yrecv, y_s, y_r, 0)

    def give(slot, value):
        ymsg[slot] = value.astype(BF16)
        returned[slot][0].start()

    @pl.when(me.two)
    def _():
        give(F2, by_rows(OWN, 2))

    yacc[F1] = by_rows(OWN, 1)
    yacc[OWN] = by_columns(OWN, 0)

    @pl.when(me.pair)
    def _():
        yacc[SIB] = by_columns(OWN, 3)

    @pl.when(me.uses_sib)
    def _():
        scaled[SIB][0].wait_recv()

        @pl.when(me.one)
        def _():
            yacc[F1] += by_rows(SIB, 2)

        @pl.when(me.pair)
        def _():
            yacc[OWN] += by_rows(SIB, 3)

    @pl.when(me.cross)
    def _():
        scaled[G][0].wait_recv()
        yacc[F1] += by_rows(G, 3)

    give(F1, yacc[F1])
    scaled[F1][0].wait_recv()

    @pl.when(me.cross)
    def _():
        give(G, by_columns(F1, 3))

    @pl.when(me.uses_sib)
    def _():
        @pl.when(jnp.logical_and(me.one, me.pair))
        def _():
            yacc[SIB] += by_columns(F1, 2)

        @pl.when(jnp.logical_and(me.one, me.cross))
        def _():
            yacc[SIB] = by_columns(F1, 2)

        give(SIB, yacc[SIB])

    yacc[OWN] += by_columns(F1, 1)

    @pl.when(me.two)
    def _():
        scaled[F2][0].wait_recv()
        yacc[OWN] += by_columns(F2, 2)

    for slot in (SIB, F2, G, F1):
        copy, _, receives = returned[slot]

        def gather(copy=copy, slot=slot):
            copy.wait_recv()
            yacc[OWN] += yrecv[slot].astype(F32)

        given(receives, gather)
    factor = 0.25 * math.sqrt((2 * ROUNDS + 1) * tiles)
    o_ref[...] = (factor * inverse) * yacc[OWN]

    for c in range(chunks):
        to_ahead(c).wait_send()
        to_sib(c).wait_send()

    @pl.when(sib.cross)
    def _():
        for c in range(chunks):
            to_g(c).wait_send()

    @pl.when(me.one)
    def _():
        for c in range(half):
            to_far(c).wait_send()
        for c in range(half, chunks):
            to_relay(c).wait_send()

    if RELAY:
        @pl.when(relayed.one)
        def _():
            for c in range(half, chunks):
                to_onward(c).wait_send()

    for group in (degrees, scaled, returned):
        for copy, sends, _ in group.values():
            given(sends, copy.wait_send)


def shards(count, features, eigvecs):
    tiles, width = features.shape
    rank = eigvecs.shape[1]
    chunks = tiles // CR
    dma = lambda n: pltpu.SemaphoreType.DMA((n,))
    out = pl.pallas_call(
        functools.partial(kernel, count),
        out_shape=jax.ShapeDtypeStruct((rank, tiles), F32),
        in_specs=[pl.BlockSpec(memory_space=pl.ANY)] * 2,
        out_specs=pl.BlockSpec(memory_space=pltpu.VMEM),
        scratch_shapes=[
            pltpu.VMEM((tiles, width), BF16),
            pltpu.VMEM((tiles, rank), BF16),
            pltpu.VMEM((5, tiles, width), BF16),
            pltpu.VMEM((tiles // 2, width), BF16),
            pltpu.VMEM((4, tiles, tiles), BF16),
            pltpu.VMEM((5, 1, tiles), F32),
            pltpu.VMEM((5, 1, tiles), F32),
            pltpu.VMEM((5, 1, tiles), F32),
            pltpu.VMEM((5, 1, tiles), F32),
            pltpu.VMEM((5, rank, tiles), BF16),
            pltpu.VMEM((5, rank, tiles), BF16),
            pltpu.VMEM((5, rank, tiles), BF16),
            pltpu.VMEM((5, rank, tiles), F32),
            dma(chunks + 1),
        ] + [dma(chunks)] * 10 + [dma(5)] * 6,
        compiler_params=pltpu.CompilerParams(
            collective_id=0, has_side_effects=True, vmem_limit_bytes=56 * 2**20
        ),
        name="cluster",
    )(features, eigvecs)
    return out.T


def solution(mesh):
    return jax.shard_map(
        functools.partial(shards, mesh.shape["dev"]),
        mesh=mesh,
        in_specs=(P("dev", None), P("dev", None)),
        out_specs=P("dev", None),
        check_vma=False,
    )
```

```python
import functools
import math

import jax
import jax.numpy as jnp
from jax import lax
from jax.experimental import pallas as pl
from jax.experimental.pallas import tpu as pltpu
from jax.sharding import PartitionSpec as P

ROUNDS = 3
MESH = pl.DeviceIdType.MESH
OWN, SIB, F1, F2, G = range(5)
CR = 256
RELAY = True
F32, BF16 = jnp.float32, jnp.bfloat16


def upward(chip, count):
    if not RELAY:
        return chip >= 0
    return chip < count // 4


class Place:
    def __init__(self, dev, count):
        wrap = lambda i: lax.rem(i + 2 * count, count)
        self.dev, self.count = dev, count
        self.core = lax.rem(dev, 2)
        chip = dev // 2
        s = 2 * self.core - 1
        self.ahead = wrap(dev + 2 * s)
        self.behind = wrap(dev - 2 * s)
        self.far = wrap(dev - 3 * s)
        self.sib = dev - s
        self.side = wrap(dev + s)
        before = lax.rem(chip + count // 2 - 1, count // 2)
        first = self.core == 0
        self.two = jnp.where(first, jnp.logical_not(upward(chip, count)), upward(before, count))
        other = jnp.where(first, upward(before, count), jnp.logical_not(upward(chip, count)))
        self.cross = jnp.where(self.two == other, self.core == 1, self.two)
        self.one = jnp.logical_not(self.two)
        self.pair = jnp.logical_not(self.cross)
        self.uses_sib = jnp.logical_or(self.one, self.pair)
        plane = count // 8
        x = chip // plane
        edge = jnp.logical_and(self.core == 1, lax.rem(chip, plane) == 0)
        flipped = jnp.where(edge, x + 1 - 2 * lax.rem(x, 2), 3 - x)
        self.relay = dev + (flipped - x) * 2 * plane
        self.s = s
        self.wrap = wrap


def kernel(count, x_hbm, e_hbm, o_ref, raw, eig, blk, rel, kst, bl, dacc, dmsg, drecv, sbuf, ymsg, yrecv, yacc,
           load_sem, sib_s, sib_r, f1_s, f1_r, f2_s, f2_r, g_s, g_r, rel_s, rel_r, d_s, d_r, v_s, v_r, y_s, y_r):
    tiles, width = raw.shape
    chunks = tiles // CR
    half = chunks // 2 if RELAY else chunks
    a = math.sqrt(2.0 * width) / width * math.log2(math.e)
    me = Place(lax.axis_index("dev"), count)
    sib = Place(me.sib, count)
    side = Place(me.side, count)

    loads = [pltpu.make_async_copy(x_hbm.at[pl.ds(c * CR, CR)], raw.at[pl.ds(c * CR, CR)], load_sem.at[c]) for c in range(chunks)]
    loads.append(pltpu.make_async_copy(e_hbm, eig, load_sem.at[chunks]))
    for load in loads:
        load.start()

    partners = [me.sib, me.ahead, me.behind, me.far, me.side]
    if RELAY:
        relayed = Place(me.relay, count)
        onward = me.wrap(me.relay - 3 * me.s)
        source = Place(me.far, count).relay
        partners += [me.relay, onward, source]
    barrier = pltpu.get_barrier_semaphore()
    for partner in partners:
        pl.semaphore_signal(barrier, inc=1, device_id=(partner,), device_id_type=MESH)

    def rows(c):
        return pl.ds(c * CR if isinstance(c, int) else pl.multiple_of(c * CR, CR), CR)

    def remote(src, dst, send, recv, to):
        return pltpu.make_async_remote_copy(src_ref=src, dst_ref=dst, send_sem=send, recv_sem=recv, device_id=(to,), device_id_type=MESH)

    def to_sib(c):
        return remote(blk.at[OWN, rows(c)], blk.at[SIB, rows(c)], sib_s.at[c], sib_r.at[c], me.sib)

    def to_ahead(c):
        return remote(blk.at[OWN, rows(c)], blk.at[F1, rows(c)], f1_s.at[c], f1_r.at[c], me.ahead)

    def to_far(c):
        return remote(blk.at[OWN, rows(c)], blk.at[F2, rows(c)], f2_s.at[c], f2_r.at[c], me.far)

    def to_relay(c):
        return remote(blk.at[OWN, rows(c)], rel.at[rows(c - half)], rel_s.at[c - half], rel_r.at[c - half], me.relay)

    def to_onward(c):
        return remote(rel.at[rows(c - half)], blk.at[F2, rows(c)], f2_s.at[c], f2_r.at[c], onward)

    def to_g(c):
        return remote(blk.at[F1, rows(c)], blk.at[G, rows(c)], g_s.at[c], g_r.at[c], me.sib)

    eye = lax.broadcasted_iota(jnp.int32, (128, 128), 0) == lax.broadcasted_iota(jnp.int32, (128, 128), 1)

    def laid(column):
        parts = []
        for start in range(0, column.shape[0], 128):
            wide = jnp.broadcast_to(column[start:start + 128], (128, 128))
            parts.append(jnp.sum(jnp.where(eye, wide, 0.0), axis=0, keepdims=True))
        return jnp.concatenate(parts, axis=1)

    def offsets(unit):
        values = unit.astype(F32)
        return (0.5 * a) * jnp.sum(values * values, axis=-1, keepdims=True)

    def normalize(c):
        values = raw[rows(c), :].astype(F32)
        mean = jnp.mean(values * values, axis=-1, keepdims=True)
        unit = (values * lax.rsqrt(mean + 1e-06)).astype(BF16)
        blk[OWN, rows(c), :] = unit
        bl[OWN, :, rows(c)] = laid(offsets(unit))

    def lay_offsets(slot):
        @pl.loop(0, chunks)
        def _(c):
            bl[slot, :, rows(c)] = laid(offsets(blk[slot, rows(c), :]))

    def tile(row_slot, c, col_slot, store, diagonal=False):
        unit = blk[row_slot, rows(c), :]
        inner = lax.dot_general(unit, blk[col_slot], (((1,), (1,)), ((), ())), preferred_element_type=F32)
        value = jnp.exp2(a * inner - offsets(unit) - bl[col_slot])
        if diagonal:
            at = lax.broadcasted_iota(jnp.int32, value.shape, 0) + c * CR
            value = jnp.where(at == lax.broadcasted_iota(jnp.int32, value.shape, 1), 0.0, value)
        kst[store, rows(c), :] = value.astype(BF16)
        dacc[col_slot] += jnp.sum(value, axis=0, keepdims=True)
        if not diagonal:
            dacc[row_slot, :, rows(c)] += laid(jnp.sum(value, axis=1, keepdims=True))

    dacc[...] = jnp.zeros_like(dacc)
    for c in range(chunks):
        loads[c].wait()
        normalize(c)
        if c == 0:
            pl.semaphore_wait(barrier, len(partners))
        to_ahead(c).start()
        if RELAY and c >= half:
            @pl.when(me.one)
            def _():
                to_relay(c).start()
        to_sib(c).start()

    loads[chunks].wait()
    yacc[0] = eig[...].astype(F32)

    @pl.loop(0, chunks)
    def _(c):
        tile(OWN, c, OWN, 0, diagonal=True)

    for c in range(chunks):
        to_sib(c).wait_recv()
    lay_offsets(SIB)

    @pl.when(me.pair)
    def _():
        @pl.loop(0, chunks)
        def _(c):
            tile(OWN, c, SIB, 3)

    @pl.loop(0, chunks)
    def _(c):
        to_ahead(c).wait_recv()

        @pl.when(sib.cross)
        def _():
            to_g(c).start()

        @pl.when(c == chunks - 2)
        def _():
            @pl.when(me.one)
            def _():
                @pl.loop(0, half)
                def _(i):
                    to_far(i).start()

            if RELAY:
                @pl.when(relayed.one)
                def _():
                    @pl.loop(half, chunks)
                    def _(i):
                        to_relay(i).wait_recv()
                        to_onward(i).start()

        tile(F1, c, OWN, 1)

        @pl.when(me.one)
        def _():
            tile(F1, c, SIB, 2)

    @pl.when(me.cross)
    def _():
        for c in range(chunks):
            to_g(c).wait_recv()
        lay_offsets(G)

        @pl.loop(0, chunks)
        def _(c):
            tile(F1, c, G, 3)

    @pl.when(me.two)
    def _():
        @pl.loop(0, chunks)
        def _(c):
            to_far(c).wait_recv()
            tile(F2, c, OWN, 2)

    def exchange(src, dst, send, recv, pick):
        holders = (
            (F1, me.behind, None, me.ahead, None),
            (G, me.side, me.cross, me.side, side.cross),
            (F2, me.far, me.two, me.far, me.one),
            (SIB, me.sib, me.uses_sib, me.sib, sib.uses_sib),
        )
        out = {}
        for slot, owner, held, holder, lent in holders:
            if pick == 0:
                out[slot] = (remote(src.at[slot], dst.at[slot], send.at[slot], recv.at[slot], owner), held, lent)
            else:
                out[slot] = (remote(src.at[OWN], dst.at[slot], send.at[slot], recv.at[slot], holder), lent, held)
        return out

    def given(condition, action):
        if condition is None:
            action()
        else:
            pl.when(condition)(action)

    degrees = exchange(dmsg, drecv, d_s, d_r, 0)
    dmsg[...] = dacc[...]
    for slot in (F1, F2, G, SIB):
        copy, sends, _ = degrees[slot]
        given(sends, copy.start)
    for slot in (SIB, G, F2, F1):
        copy, _, receives = degrees[slot]

        def add(copy=copy, slot=slot):
            copy.wait_recv()
            dacc[OWN] += drecv[slot]

        given(receives, add)
    inverse = lax.rsqrt(dacc[OWN])
    sbuf[OWN] = (yacc[0] * inverse).astype(BF16)

    scaled = exchange(sbuf, sbuf, v_s, v_r, 1)
    for slot in (G, F1, F2, SIB):
        copy, sends, _ = scaled[slot]
        given(sends, copy.start)

    def by_columns(slot, store):
        return jnp.dot(sbuf[slot], kst[store], preferred_element_type=F32)

    def by_rows(slot, store):
        return lax.dot_general(sbuf[slot], kst[store], (((1,), (1,)), ((), ())), preferred_element_type=F32)

    returned = exchange(ymsg, yrecv, y_s, y_r, 0)

    def give(slot, value):
        ymsg[slot] = value.astype(BF16)
        returned[slot][0].start()

    @pl.when(me.two)
    def _():
        give(F2, by_rows(OWN, 2))

    yacc[F1] = by_rows(OWN, 1)
    yacc[OWN] = by_columns(OWN, 0)

    @pl.when(me.pair)
    def _():
        yacc[SIB] = by_columns(OWN, 3)

    @pl.when(me.uses_sib)
    def _():
        scaled[SIB][0].wait_recv()

        @pl.when(me.one)
        def _():
            yacc[F1] += by_rows(SIB, 2)

        @pl.when(me.pair)
        def _():
            yacc[OWN] += by_rows(SIB, 3)

    @pl.when(me.cross)
    def _():
        scaled[G][0].wait_recv()
        yacc[F1] += by_rows(G, 3)

    give(F1, yacc[F1])
    scaled[F1][0].wait_recv()

    @pl.when(me.cross)
    def _():
        give(G, by_columns(F1, 3))

    @pl.when(me.uses_sib)
    def _():
        @pl.when(jnp.logical_and(me.one, me.pair))
        def _():
            yacc[SIB] += by_columns(F1, 2)

        @pl.when(jnp.logical_and(me.one, me.cross))
        def _():
            yacc[SIB] = by_columns(F1, 2)

        give(SIB, yacc[SIB])

    yacc[OWN] += by_columns(F1, 1)

    @pl.when(me.two)
    def _():
        scaled[F2][0].wait_recv()
        yacc[OWN] += by_columns(F2, 2)

    for slot in (SIB, F2, G, F1):
        copy, _, receives = returned[slot]

        def gather(copy=copy, slot=slot):
            copy.wait_recv()
            yacc[OWN] += yrecv[slot].astype(F32)

        given(receives, gather)
    factor = 0.25 * math.sqrt((2 * ROUNDS + 1) * tiles)
    o_ref[...] = (factor * inverse) * yacc[OWN]

    for c in range(chunks):
        to_ahead(c).wait_send()
        to_sib(c).wait_send()

    @pl.when(sib.cross)
    def _():
        for c in range(chunks):
            to_g(c).wait_send()

    @pl.when(me.one)
    def _():
        for c in range(half):
            to_far(c).wait_send()
        for c in range(half, chunks):
            to_relay(c).wait_send()

    if RELAY:
        @pl.when(relayed.one)
        def _():
            for c in range(half, chunks):
                to_onward(c).wait_send()

    for group in (degrees, scaled, returned):
        for copy, sends, _ in group.values():
            given(sends, copy.wait_send)


def shards(count, features, eigvecs):
    tiles, width = features.shape
    rank = eigvecs.shape[1]
    chunks = tiles // CR
    dma = lambda n: pltpu.SemaphoreType.DMA((n,))
    out = pl.pallas_call(
        functools.partial(kernel, count),
        out_shape=jax.ShapeDtypeStruct((rank, tiles), F32),
        in_specs=[pl.BlockSpec(memory_space=pl.ANY)] * 2,
        out_specs=pl.BlockSpec(memory_space=pltpu.VMEM),
        scratch_shapes=[
            pltpu.VMEM((tiles, width), BF16),
            pltpu.VMEM((rank, tiles), BF16),
            pltpu.VMEM((5, tiles, width), BF16),
            pltpu.VMEM((tiles // 2, width), BF16),
            pltpu.VMEM((4, tiles, tiles), BF16),
            pltpu.VMEM((5, 1, tiles), F32),
            pltpu.VMEM((5, 1, tiles), F32),
            pltpu.VMEM((5, 1, tiles), F32),
            pltpu.VMEM((5, 1, tiles), F32),
            pltpu.VMEM((5, rank, tiles), BF16),
            pltpu.VMEM((5, rank, tiles), BF16),
            pltpu.VMEM((5, rank, tiles), BF16),
            pltpu.VMEM((5, rank, tiles), F32),
            dma(chunks + 1),
        ] + [dma(chunks)] * 10 + [dma(5)] * 6,
        compiler_params=pltpu.CompilerParams(
            collective_id=0, has_side_effects=True, vmem_limit_bytes=56 * 2**20
        ),
        name="cluster",
    )(features, eigvecs.T)
    return out.T


def solution(mesh):
    return jax.shard_map(
        functools.partial(shards, mesh.shape["dev"]),
        mesh=mesh,
        in_specs=(P("dev", None), P("dev", None)),
        out_specs=P("dev", None),
        check_vma=False,
    )
```

```python
import functools
import math

import jax
import jax.numpy as jnp
from jax import lax
from jax.experimental import pallas as pl
from jax.experimental.pallas import tpu as pltpu
from jax.sharding import PartitionSpec as P

ROUNDS = 3
MESH = pl.DeviceIdType.MESH
OWN, SIB, F1, F2, G = range(5)
CR = 256
DIMS = (4, 4, 8)
F32, BF16 = jnp.float32, jnp.bfloat16


def upward(chip):
    x, y, z = chip // (DIMS[1] * DIMS[2]), lax.rem(chip // DIMS[2], DIMS[1]), lax.rem(chip, DIMS[2])
    return jnp.where(z < DIMS[2] - 1, x < DIMS[0] // 2, lax.rem(y, 2) == 0)


class Place:
    def __init__(self, dev, count):
        wrap = lambda i: lax.rem(i + 2 * count, count)
        self.dev, self.count, self.wrap = dev, count, wrap
        core = lax.rem(dev, 2)
        chip = dev // 2
        s = 2 * core - 1
        self.s = s
        self.ahead = wrap(dev + 2 * s)
        self.behind = wrap(dev - 2 * s)
        self.far = wrap(dev - 3 * s)
        self.sib = dev - s
        self.side = wrap(dev + s)
        before = lax.rem(chip + count // 2 - 1, count // 2)
        first = core == 0
        self.two = jnp.where(first, jnp.logical_not(upward(chip)), upward(before))
        other = jnp.where(first, upward(before), jnp.logical_not(upward(chip)))
        self.cross = jnp.where(self.two == other, core == 1, self.two)
        self.one = jnp.logical_not(self.two)
        self.pair = jnp.logical_not(self.cross)
        self.uses_sib = jnp.logical_or(self.one, self.pair)
        x, y, z = chip // (DIMS[1] * DIMS[2]), lax.rem(chip // DIMS[2], DIMS[1]), lax.rem(chip, DIMS[2])
        turn = jnp.where(first, z == DIMS[2] - 1, z == 0)
        across = dev + (DIMS[0] - 1 - 2 * x) * (2 * DIMS[1] * DIMS[2])
        self.relay = jnp.where(turn, wrap(dev - s * 2 * DIMS[2]), across)
        self.source = jnp.where(turn, wrap(dev + s * 2 * DIMS[2]), across)
        low = z - core
        kept = jnp.logical_and(
            jnp.logical_or(y == 0, y == DIMS[1] - 1),
            jnp.logical_or(low == 0, low == DIMS[2] - 2),
        )
        self.split = jnp.logical_and(self.one, jnp.logical_or(turn, jnp.logical_not(kept)))


def kernel(count, x_hbm, e_hbm, o_ref, raw, eig, blk, rel, kst, bl, dacc, dmsg, drecv, sbuf, ymsg, yrecv, yacc,
           load_sem, sib_s, sib_r, f1_s, f1_r, f2_s, f2_r, g_s, g_r, rel_s, rel_r, d_s, d_r, v_s, v_r, y_s, y_r):
    tiles, width = raw.shape
    chunks = tiles // CR
    half = chunks // 2
    a = math.sqrt(2.0 * width) / width * math.log2(math.e)
    me = Place(lax.axis_index("dev"), count)
    sib = Place(me.sib, count)
    side = Place(me.side, count)

    loads = [pltpu.make_async_copy(x_hbm.at[pl.ds(c * CR, CR)], raw.at[pl.ds(c * CR, CR)], load_sem.at[c]) for c in range(chunks)]
    loads.append(pltpu.make_async_copy(e_hbm, eig, load_sem.at[chunks]))
    for load in loads:
        load.start()

    partners = [me.sib, me.ahead, me.behind, me.far, me.side]
    source = Place(me.source, count)
    onward = source.far
    partners += [me.relay, me.source, onward, Place(me.far, count).relay]
    barrier = pltpu.get_barrier_semaphore()
    for partner in partners:
        pl.semaphore_signal(barrier, inc=1, device_id=(partner,), device_id_type=MESH)

    def rows(c):
        return pl.ds(c * CR if isinstance(c, int) else pl.multiple_of(c * CR, CR), CR)

    def remote(src, dst, send, recv, to):
        return pltpu.make_async_remote_copy(src_ref=src, dst_ref=dst, send_sem=send, recv_sem=recv, device_id=(to,), device_id_type=MESH)

    def to_sib(c):
        return remote(blk.at[OWN, rows(c)], blk.at[SIB, rows(c)], sib_s.at[c], sib_r.at[c], me.sib)

    def to_ahead(c):
        return remote(blk.at[OWN, rows(c)], blk.at[F1, rows(c)], f1_s.at[c], f1_r.at[c], me.ahead)

    def to_far(c):
        return remote(blk.at[OWN, rows(c)], blk.at[F2, rows(c)], f2_s.at[c], f2_r.at[c], me.far)

    def to_relay(c):
        return remote(blk.at[OWN, rows(c)], rel.at[rows(c - half)], rel_s.at[c - half], rel_r.at[c - half], me.relay)

    def to_onward(c):
        return remote(rel.at[rows(c - half)], blk.at[F2, rows(c)], f2_s.at[c], f2_r.at[c], onward)

    def to_g(c):
        return remote(blk.at[F1, rows(c)], blk.at[G, rows(c)], g_s.at[c], g_r.at[c], me.sib)

    eye = lax.broadcasted_iota(jnp.int32, (128, 128), 0) == lax.broadcasted_iota(jnp.int32, (128, 128), 1)

    def laid(column):
        parts = []
        for start in range(0, column.shape[0], 128):
            wide = jnp.broadcast_to(column[start:start + 128], (128, 128))
            parts.append(jnp.sum(jnp.where(eye, wide, 0.0), axis=0, keepdims=True))
        return jnp.concatenate(parts, axis=1)

    def offsets(unit):
        values = unit.astype(F32)
        return (0.5 * a) * jnp.sum(values * values, axis=-1, keepdims=True)

    def normalize(c):
        values = raw[rows(c), :].astype(F32)
        mean = jnp.mean(values * values, axis=-1, keepdims=True)
        unit = (values * lax.rsqrt(mean + 1e-06)).astype(BF16)
        blk[OWN, rows(c), :] = unit
        bl[OWN, :, rows(c)] = laid(offsets(unit))

    def lay_offsets(slot):
        @pl.loop(0, chunks)
        def _(c):
            bl[slot, :, rows(c)] = laid(offsets(blk[slot, rows(c), :]))

    def tile(row_slot, c, col_slot, store, diagonal=False):
        unit = blk[row_slot, rows(c), :]
        inner = lax.dot_general(unit, blk[col_slot], (((1,), (1,)), ((), ())), preferred_element_type=F32)
        value = jnp.exp2(a * inner - offsets(unit) - bl[col_slot])
        if diagonal:
            at = lax.broadcasted_iota(jnp.int32, value.shape, 0) + c * CR
            value = jnp.where(at == lax.broadcasted_iota(jnp.int32, value.shape, 1), 0.0, value)
        kst[store, rows(c), :] = value.astype(BF16)
        dacc[col_slot] += jnp.sum(value, axis=0, keepdims=True)
        if not diagonal:
            dacc[row_slot, :, rows(c)] += laid(jnp.sum(value, axis=1, keepdims=True))

    dacc[...] = jnp.zeros_like(dacc)
    for c in range(chunks):
        loads[c].wait()
        normalize(c)
        if c == 0:
            pl.semaphore_wait(barrier, len(partners))
        to_ahead(c).start()
        if c >= half:
            @pl.when(me.split)
            def _():
                to_relay(c).start()
        to_sib(c).start()

    loads[chunks].wait()
    yacc[0] = eig[...].astype(F32)

    @pl.loop(0, chunks)
    def _(c):
        tile(OWN, c, OWN, 0, diagonal=True)

    for c in range(chunks):
        to_sib(c).wait_recv()
    lay_offsets(SIB)

    @pl.when(me.pair)
    def _():
        @pl.loop(0, chunks)
        def _(c):
            tile(OWN, c, SIB, 3)

    @pl.loop(0, chunks)
    def _(c):
        to_ahead(c).wait_recv()

        @pl.when(sib.cross)
        def _():
            to_g(c).start()

        @pl.when(c == chunks - 2)
        def _():
            @pl.when(me.one)
            def _():
                @pl.loop(0, half)
                def _(i):
                    to_far(i).start()

            @pl.when(me.one & jnp.logical_not(me.split))
            def _():
                @pl.loop(half, chunks)
                def _(i):
                    to_far(i).start()

            @pl.when(source.split)
            def _():
                @pl.loop(half, chunks)
                def _(i):
                    to_relay(i).wait_recv()
                    to_onward(i).start()

        tile(F1, c, OWN, 1)

        @pl.when(me.one)
        def _():
            tile(F1, c, SIB, 2)

    @pl.when(me.cross)
    def _():
        for c in range(chunks):
            to_g(c).wait_recv()
        lay_offsets(G)

        @pl.loop(0, chunks)
        def _(c):
            tile(F1, c, G, 3)

    @pl.when(me.two)
    def _():
        @pl.loop(0, chunks)
        def _(i):
            c = i // 2 + lax.rem(i, 2) * half
            to_far(c).wait_recv()
            tile(F2, c, OWN, 2)

    def exchange(src, dst, send, recv, pick):
        holders = (
            (F1, me.behind, None, me.ahead, None),
            (G, me.side, me.cross, me.side, side.cross),
            (F2, me.far, me.two, me.far, me.one),
            (SIB, me.sib, me.uses_sib, me.sib, sib.uses_sib),
        )
        out = {}
        for slot, owner, held, holder, lent in holders:
            if pick == 0:
                out[slot] = (remote(src.at[slot], dst.at[slot], send.at[slot], recv.at[slot], owner), held, lent)
            else:
                out[slot] = (remote(src.at[OWN], dst.at[slot], send.at[slot], recv.at[slot], holder), lent, held)
        return out

    def given(condition, action):
        if condition is None:
            action()
        else:
            pl.when(condition)(action)

    degrees = exchange(dmsg, drecv, d_s, d_r, 0)
    dmsg[...] = dacc[...]
    for slot in (F1, F2, G, SIB):
        copy, sends, _ = degrees[slot]
        given(sends, copy.start)
    for slot in (SIB, G, F2, F1):
        copy, _, receives = degrees[slot]

        def add(copy=copy, slot=slot):
            copy.wait_recv()
            dacc[OWN] += drecv[slot]

        given(receives, add)
    inverse = lax.rsqrt(dacc[OWN])
    sbuf[OWN] = (yacc[0] * inverse).astype(BF16)

    scaled = exchange(sbuf, sbuf, v_s, v_r, 1)
    for slot in (G, F1, F2, SIB):
        copy, sends, _ = scaled[slot]
        given(sends, copy.start)

    def by_columns(slot, store):
        return jnp.dot(sbuf[slot], kst[store], preferred_element_type=F32)

    def by_rows(slot, store):
        return lax.dot_general(sbuf[slot], kst[store], (((1,), (1,)), ((), ())), preferred_element_type=F32)

    returned = exchange(ymsg, yrecv, y_s, y_r, 0)

    def give(slot, value):
        ymsg[slot] = value.astype(BF16)
        returned[slot][0].start()

    @pl.when(me.two)
    def _():
        give(F2, by_rows(OWN, 2))

    yacc[F1] = by_rows(OWN, 1)
    yacc[OWN] = by_columns(OWN, 0)

    @pl.when(me.pair)
    def _():
        yacc[SIB] = by_columns(OWN, 3)

    @pl.when(me.uses_sib)
    def _():
        scaled[SIB][0].wait_recv()

        @pl.when(me.one)
        def _():
            yacc[F1] += by_rows(SIB, 2)

        @pl.when(me.pair)
        def _():
            yacc[OWN] += by_rows(SIB, 3)

    @pl.when(me.cross)
    def _():
        scaled[G][0].wait_recv()
        yacc[F1] += by_rows(G, 3)

    give(F1, yacc[F1])
    scaled[F1][0].wait_recv()

    @pl.when(me.cross)
    def _():
        give(G, by_columns(F1, 3))

    @pl.when(me.uses_sib)
    def _():
        @pl.when(jnp.logical_and(me.one, me.pair))
        def _():
            yacc[SIB] += by_columns(F1, 2)

        @pl.when(jnp.logical_and(me.one, me.cross))
        def _():
            yacc[SIB] = by_columns(F1, 2)

        give(SIB, yacc[SIB])

    yacc[OWN] += by_columns(F1, 1)

    @pl.when(me.two)
    def _():
        scaled[F2][0].wait_recv()
        yacc[OWN] += by_columns(F2, 2)

    for slot in (SIB, F2, G, F1):
        copy, _, receives = returned[slot]

        def gather(copy=copy, slot=slot):
            copy.wait_recv()
            yacc[OWN] += yrecv[slot].astype(F32)

        given(receives, gather)
    factor = 0.25 * math.sqrt((2 * ROUNDS + 1) * tiles)
    o_ref[...] = (factor * inverse) * yacc[OWN]

    for c in range(chunks):
        to_ahead(c).wait_send()
        to_sib(c).wait_send()

    @pl.when(sib.cross)
    def _():
        for c in range(chunks):
            to_g(c).wait_send()

    @pl.when(me.one)
    def _():
        for c in range(half):
            to_far(c).wait_send()

    @pl.when(me.one & jnp.logical_not(me.split))
    def _():
        for c in range(half, chunks):
            to_far(c).wait_send()

    @pl.when(me.split)
    def _():
        for c in range(half, chunks):
            to_relay(c).wait_send()

    @pl.when(source.split)
    def _():
        for c in range(half, chunks):
            to_onward(c).wait_send()

    for group in (degrees, scaled, returned):
        for copy, sends, _ in group.values():
            given(sends, copy.wait_send)


def shards(count, features, eigvecs):
    tiles, width = features.shape
    rank = eigvecs.shape[1]
    chunks = tiles // CR
    dma = lambda n: pltpu.SemaphoreType.DMA((n,))
    out = pl.pallas_call(
        functools.partial(kernel, count),
        out_shape=jax.ShapeDtypeStruct((rank, tiles), F32),
        in_specs=[pl.BlockSpec(memory_space=pl.ANY)] * 2,
        out_specs=pl.BlockSpec(memory_space=pltpu.VMEM),
        scratch_shapes=[
            pltpu.VMEM((tiles, width), BF16),
            pltpu.VMEM((rank, tiles), BF16),
            pltpu.VMEM((5, tiles, width), BF16),
            pltpu.VMEM((tiles // 2, width), BF16),
            pltpu.VMEM((4, tiles, tiles), BF16),
            pltpu.VMEM((5, 1, tiles), F32),
            pltpu.VMEM((5, 1, tiles), F32),
            pltpu.VMEM((5, 1, tiles), F32),
            pltpu.VMEM((5, 1, tiles), F32),
            pltpu.VMEM((5, rank, tiles), BF16),
            pltpu.VMEM((5, rank, tiles), BF16),
            pltpu.VMEM((5, rank, tiles), BF16),
            pltpu.VMEM((5, rank, tiles), F32),
            dma(chunks + 1),
        ] + [dma(chunks)] * 10 + [dma(5)] * 6,
        compiler_params=pltpu.CompilerParams(
            collective_id=0, has_side_effects=True, vmem_limit_bytes=56 * 2**20
        ),
        name="cluster",
    )(features, eigvecs.T)
    return out.T


def solution(mesh):
    return jax.shard_map(
        functools.partial(shards, mesh.shape["dev"]),
        mesh=mesh,
        in_specs=(P("dev", None), P("dev", None)),
        out_specs=P("dev", None),
        check_vma=False,
    )
```

```python
import functools
import math

import jax
import jax.numpy as jnp
from jax import lax
from jax.experimental import pallas as pl
from jax.experimental.pallas import tpu as pltpu
from jax.sharding import PartitionSpec as P

ROUNDS = 3
MESH = pl.DeviceIdType.MESH
OWN, SIB, F1, F2, G = range(5)
CR = 256
DIMS = (4, 4, 8)
F32, BF16 = jnp.float32, jnp.bfloat16


def upward(chip):
    x, y, z = chip // (DIMS[1] * DIMS[2]), lax.rem(chip // DIMS[2], DIMS[1]), lax.rem(chip, DIMS[2])
    outer = (y == 0) | (y == DIMS[1] - 1)
    middle = (x == DIMS[0] // 2 - 1) | (x == DIMS[0] // 2)
    return jnp.where(z < DIMS[2] - 1, (x < DIMS[0] // 2) != (outer & middle), lax.rem(y, 2) == 0)


class Place:
    def __init__(self, dev, count):
        wrap = lambda i: lax.rem(i + 2 * count, count)
        self.dev, self.count, self.wrap = dev, count, wrap
        core = lax.rem(dev, 2)
        chip = dev // 2
        s = 2 * core - 1
        self.s = s
        self.ahead = wrap(dev + 2 * s)
        self.behind = wrap(dev - 2 * s)
        self.far = wrap(dev - 3 * s)
        self.sib = dev - s
        self.side = wrap(dev + s)
        before = lax.rem(chip + count // 2 - 1, count // 2)
        first = core == 0
        self.two = jnp.where(first, jnp.logical_not(upward(chip)), upward(before))
        other = jnp.where(first, upward(before), jnp.logical_not(upward(chip)))
        self.cross = jnp.where(self.two == other, core == 1, self.two)
        self.one = jnp.logical_not(self.two)
        self.pair = jnp.logical_not(self.cross)
        self.uses_sib = jnp.logical_or(self.one, self.pair)
        x, y, z = chip // (DIMS[1] * DIMS[2]), lax.rem(chip // DIMS[2], DIMS[1]), lax.rem(chip, DIMS[2])
        turn = jnp.where(first, z == DIMS[2] - 1, z == 0)
        across = dev + (DIMS[0] - 1 - 2 * x) * (2 * DIMS[1] * DIMS[2])
        self.relay = jnp.where(turn, wrap(dev - s * 2 * DIMS[2]), across)
        self.source = jnp.where(turn, wrap(dev + s * 2 * DIMS[2]), across)


def kernel(count, x_hbm, e_hbm, o_ref, raw, blk, rel, kst, bl, dacc, total, drecv, ebuf, sbuf, ymsg, yrecv, yacc,
           load_sem, sib_s, sib_r, f1_s, f1_r, f2_s, f2_r, g_s, g_r, rel_s, rel_r, e_s, e_r, y_s, y_r, d_s, d_r):
    tiles, width = raw.shape
    chunks = tiles // CR
    half = chunks // 2
    a = math.sqrt(2.0 * width) / width * math.log2(math.e)
    me = Place(lax.axis_index("dev"), count)
    sib = Place(me.sib, count)
    side = Place(me.side, count)

    loads = [pltpu.make_async_copy(x_hbm.at[pl.ds(c * CR, CR)], raw.at[pl.ds(c * CR, CR)], load_sem.at[c]) for c in range(chunks)]
    loads.append(pltpu.make_async_copy(e_hbm, ebuf.at[OWN], load_sem.at[chunks]))
    for load in loads:
        load.start()

    partners = [me.wrap(me.dev + step) for step in (1, -1, 2, -2, 3, -3, 4, -4, 5, -5)]
    source = Place(me.source, count)
    onward = source.far
    partners += [me.relay, me.source, onward, Place(me.far, count).relay]
    barrier = pltpu.get_barrier_semaphore()
    for partner in partners:
        pl.semaphore_signal(barrier, inc=1, device_id=(partner,), device_id_type=MESH)

    def rows(c):
        return pl.ds(c * CR if isinstance(c, int) else pl.multiple_of(c * CR, CR), CR)

    def remote(src, dst, send, recv, to):
        return pltpu.make_async_remote_copy(src_ref=src, dst_ref=dst, send_sem=send, recv_sem=recv, device_id=(to,), device_id_type=MESH)

    def to_sib(c):
        return remote(blk.at[OWN, rows(c)], blk.at[SIB, rows(c)], sib_s.at[c], sib_r.at[c], me.sib)

    def to_ahead(c):
        return remote(blk.at[OWN, rows(c)], blk.at[F1, rows(c)], f1_s.at[c], f1_r.at[c], me.ahead)

    def to_far(c):
        return remote(blk.at[OWN, rows(c)], blk.at[F2, rows(c)], f2_s.at[c], f2_r.at[c], me.far)

    def to_relay(c):
        return remote(blk.at[OWN, rows(c)], rel.at[rows(c - half)], rel_s.at[c - half], rel_r.at[c - half], me.relay)

    def to_onward(c):
        return remote(rel.at[rows(c - half)], blk.at[F2, rows(c)], f2_s.at[c], f2_r.at[c], onward)

    def to_g(c):
        return remote(blk.at[F1, rows(c)], blk.at[G, rows(c)], g_s.at[c], g_r.at[c], me.sib)

    eye = lax.broadcasted_iota(jnp.int32, (128, 128), 0) == lax.broadcasted_iota(jnp.int32, (128, 128), 1)

    def laid(column):
        parts = []
        for start in range(0, column.shape[0], 128):
            wide = jnp.broadcast_to(column[start:start + 128], (128, 128))
            parts.append(jnp.sum(jnp.where(eye, wide, 0.0), axis=0, keepdims=True))
        return jnp.concatenate(parts, axis=1)

    def offsets(unit):
        values = unit.astype(F32)
        return (0.5 * a) * jnp.sum(values * values, axis=-1, keepdims=True)

    def normalize(c):
        values = raw[rows(c), :].astype(F32)
        mean = jnp.mean(values * values, axis=-1, keepdims=True)
        unit = (values * lax.rsqrt(mean + 1e-06)).astype(BF16)
        blk[OWN, rows(c), :] = unit
        bl[OWN, :, rows(c)] = laid(offsets(unit))

    def lay_offsets(slot):
        @pl.loop(0, chunks)
        def _(c):
            bl[slot, :, rows(c)] = laid(offsets(blk[slot, rows(c), :]))

    def tile(row_slot, c, col_slot, store, diagonal=False):
        unit = blk[row_slot, rows(c), :]
        inner = lax.dot_general(unit, blk[col_slot], (((1,), (1,)), ((), ())), preferred_element_type=F32)
        value = jnp.exp2(a * inner - offsets(unit) - bl[col_slot])
        if diagonal:
            at = lax.broadcasted_iota(jnp.int32, value.shape, 0) + c * CR
            value = jnp.where(at == lax.broadcasted_iota(jnp.int32, value.shape, 1), 0.0, value)
        kst[store, rows(c), :] = value.astype(BF16)
        dacc[col_slot] += jnp.sum(value, axis=0, keepdims=True)
        if not diagonal:
            dacc[row_slot, :, rows(c)] += laid(jnp.sum(value, axis=1, keepdims=True))

    dacc[...] = jnp.zeros_like(dacc)
    for c in range(chunks):
        loads[c].wait()
        normalize(c)
        if c == 0:
            pl.semaphore_wait(barrier, len(partners))
        to_ahead(c).start()
        if c >= half:
            @pl.when(me.one)
            def _():
                to_relay(c).start()
        to_sib(c).start()

    loads[chunks].wait()

    def eig_to(slot, to):
        return remote(ebuf.at[OWN], ebuf.at[slot], e_s.at[slot], e_r.at[slot], to)

    eig_ahead, eig_far, eig_sib = eig_to(F1, me.ahead), eig_to(F2, me.far), eig_to(SIB, me.sib)
    eig_g = remote(ebuf.at[F1], ebuf.at[G], e_s.at[G], e_r.at[G], me.sib)
    eig_ahead.start()

    @pl.when(sib.uses_sib)
    def _():
        eig_sib.start()

    @pl.loop(0, chunks)
    def _(c):
        tile(OWN, c, OWN, 0, diagonal=True)

    for c in range(chunks):
        to_sib(c).wait_recv()
    lay_offsets(SIB)

    @pl.when(me.pair)
    def _():
        @pl.loop(0, chunks)
        def _(c):
            tile(OWN, c, SIB, 3)

    @pl.loop(0, chunks)
    def _(c):
        to_ahead(c).wait_recv()

        @pl.when(sib.cross)
        def _():
            to_g(c).start()

        @pl.when(c == chunks - 2)
        def _():
            @pl.when(me.one)
            def _():
                eig_far.start()

                @pl.loop(0, half)
                def _(i):
                    to_far(i).start()

            @pl.when(source.one)
            def _():
                @pl.loop(half, chunks)
                def _(i):
                    to_relay(i).wait_recv()
                    to_onward(i).start()

        tile(F1, c, OWN, 1)

        @pl.when(me.one)
        def _():
            tile(F1, c, SIB, 2)

    eig_ahead.wait_recv()

    @pl.when(sib.cross)
    def _():
        eig_g.start()

    @pl.when(me.cross)
    def _():
        for c in range(chunks):
            to_g(c).wait_recv()
        lay_offsets(G)

        @pl.loop(0, chunks)
        def _(c):
            tile(F1, c, G, 3)

    owners = {OWN: me, F1: Place(me.behind, count), G: side, F2: Place(me.far, count), SIB: sib}
    held = {OWN: None, F1: None, G: me.cross, F2: me.two, SIB: me.uses_sib}

    def member(owner, kind):
        if kind == OWN:
            return owner.dev, None
        if kind == F1:
            return owner.ahead, None
        if kind == G:
            return owner.side, Place(owner.side, count).cross
        if kind == F2:
            return owner.far, owner.one
        return owner.sib, Place(owner.sib, count).uses_sib

    def given(conditions, action):
        known = [c for c in conditions if c is not None]
        if known:
            pl.when(functools.reduce(jnp.logical_and, known))(action)
        else:
            action()

    def part(slot, kind):
        dev, exists = member(owners[slot], kind)
        out = lambda: remote(dacc.at[slot], drecv.at[kind, slot], d_s.at[slot, kind], d_r.at[kind, slot], dev)
        back = lambda: remote(dacc.at[kind], drecv.at[slot, kind], d_s.at[kind, slot], d_r.at[slot, kind], dev)
        return out, back, (held[slot], exists)

    kinds = (OWN, F1, G, F2, SIB)

    def send_parts(slot):
        for kind in kinds:
            if kind != slot:
                out, _, when = part(slot, kind)
                given(when, lambda: out().start())

    send_parts(F1)
    send_parts(G)
    send_parts(SIB)

    @pl.when(me.two)
    def _():
        @pl.loop(0, chunks)
        def _(i):
            c = i // 2 + lax.rem(i, 2) * half
            to_far(c).wait_recv()
            tile(F2, c, OWN, 2)

    send_parts(OWN)
    send_parts(F2)

    def scale(slot):
        for kind in kinds:
            if kind != slot:
                _, back, when = part(slot, kind)

                def add(back=back, kind=kind):
                    back().wait_recv()
                    total[slot] += drecv[slot, kind]

                given(when, add)
        inverse = lax.rsqrt(total[slot])
        sbuf[slot] = (ebuf[slot].astype(F32) * inverse).astype(BF16)

    def by_columns(slot, store):
        return jnp.dot(sbuf[slot], kst[store], preferred_element_type=F32)

    def by_rows(slot, store):
        return lax.dot_general(sbuf[slot], kst[store], (((1,), (1,)), ((), ())), preferred_element_type=F32)

    def returns(slot):
        out = remote(ymsg.at[slot], yrecv.at[slot], y_s.at[slot], y_r.at[slot], owners[slot].dev)
        return out, held[slot], member(me, slot)[1]

    def give(slot, value):
        ymsg[slot] = value.astype(BF16)
        returns(slot)[0].start()

    total[...] = dacc[...]
    scale(OWN)

    @pl.when(me.two)
    def _():
        give(F2, by_rows(OWN, 2))

    yacc[F1] = by_rows(OWN, 1)

    @pl.when(me.uses_sib)
    def _():
        eig_sib.wait_recv()
        scale(SIB)

        @pl.when(me.one)
        def _():
            yacc[F1] += by_rows(SIB, 2)

    @pl.when(me.cross)
    def _():
        eig_g.wait_recv()
        scale(G)
        yacc[F1] += by_rows(G, 3)

    give(F1, yacc[F1])
    scale(F1)

    @pl.when(me.cross)
    def _():
        give(G, by_columns(F1, 3))

    @pl.when(me.uses_sib)
    def _():
        yacc[SIB] = jnp.zeros_like(yacc[SIB])

        @pl.when(me.one)
        def _():
            yacc[SIB] += by_columns(F1, 2)

        @pl.when(me.pair)
        def _():
            yacc[SIB] += by_columns(OWN, 3)

        give(SIB, yacc[SIB])

    yacc[OWN] = by_columns(OWN, 0)
    yacc[OWN] += by_columns(F1, 1)

    @pl.when(me.two)
    def _():
        eig_far.wait_recv()
        scale(F2)
        yacc[OWN] += by_columns(F2, 2)

    @pl.when(me.pair)
    def _():
        yacc[OWN] += by_rows(SIB, 3)

    for slot in (SIB, F2, G, F1):
        copy, _, receives = returns(slot)

        def gather(copy=copy, slot=slot):
            copy.wait_recv()
            yacc[OWN] += yrecv[slot].astype(F32)

        given((receives,), gather)
    inverse = lax.rsqrt(total[OWN])
    factor = 0.25 * math.sqrt((2 * ROUNDS + 1) * tiles)
    o_ref[...] = (factor * inverse) * yacc[OWN]

    for c in range(chunks):
        to_ahead(c).wait_send()
        to_sib(c).wait_send()

    @pl.when(sib.cross)
    def _():
        for c in range(chunks):
            to_g(c).wait_send()

    @pl.when(me.one)
    def _():
        for c in range(half):
            to_far(c).wait_send()

    @pl.when(me.one)
    def _():
        for c in range(half, chunks):
            to_relay(c).wait_send()

    @pl.when(source.one)
    def _():
        for c in range(half, chunks):
            to_onward(c).wait_send()

    eig_ahead.wait_send()
    given((sib.uses_sib,), eig_sib.wait_send)
    given((me.one,), eig_far.wait_send)
    given((sib.cross,), eig_g.wait_send)
    for slot in kinds:
        for kind in kinds:
            if kind != slot:
                out, _, when = part(slot, kind)
                given(when, lambda: out().wait_send())
        if slot != OWN:
            copy, sends, _ = returns(slot)
            given((sends,), copy.wait_send)


def shards(count, features, eigvecs):
    tiles, width = features.shape
    rank = eigvecs.shape[1]
    chunks = tiles // CR
    dma = lambda n: pltpu.SemaphoreType.DMA((n,))
    out = pl.pallas_call(
        functools.partial(kernel, count),
        out_shape=jax.ShapeDtypeStruct((rank, tiles), F32),
        in_specs=[pl.BlockSpec(memory_space=pl.ANY)] * 2,
        out_specs=pl.BlockSpec(memory_space=pltpu.VMEM),
        scratch_shapes=[
            pltpu.VMEM((tiles, width), BF16),
            pltpu.VMEM((5, tiles, width), BF16),
            pltpu.VMEM((tiles // 2, width), BF16),
            pltpu.VMEM((4, tiles, tiles), BF16),
            pltpu.VMEM((5, 1, tiles), F32),
            pltpu.VMEM((5, 1, tiles), F32),
            pltpu.VMEM((5, 1, tiles), F32),
            pltpu.VMEM((5, 5, 1, tiles), F32),
            pltpu.VMEM((5, rank, tiles), BF16),
            pltpu.VMEM((5, rank, tiles), BF16),
            pltpu.VMEM((5, rank, tiles), BF16),
            pltpu.VMEM((5, rank, tiles), BF16),
            pltpu.VMEM((5, rank, tiles), F32),
            dma(chunks + 1),
        ] + [dma(chunks)] * 10 + [dma(5)] * 4 + [pltpu.SemaphoreType.DMA((5, 5))] * 2,
        compiler_params=pltpu.CompilerParams(
            collective_id=0, has_side_effects=True, vmem_limit_bytes=56 * 2**20
        ),
        name="cluster",
    )(features, eigvecs.T)
    return out.T


def solution(mesh):
    return jax.shard_map(
        functools.partial(shards, mesh.shape["dev"]),
        mesh=mesh,
        in_specs=(P("dev", None), P("dev", None)),
        out_specs=P("dev", None),
        check_vma=False,
    )
```

```python
import functools
import math

import jax
import jax.numpy as jnp
from jax import lax
from jax.experimental import pallas as pl
from jax.experimental.pallas import tpu as pltpu
from jax.sharding import PartitionSpec as P

ROUNDS = 3
MESH = pl.DeviceIdType.MESH
OWN, SIB, F1, F2, G = range(5)
CR = 256
DIMS = (4, 4, 8)
F32, BF16 = jnp.float32, jnp.bfloat16


def upward(chip):
    x, y, z = chip // (DIMS[1] * DIMS[2]), lax.rem(chip // DIMS[2], DIMS[1]), lax.rem(chip, DIMS[2])
    outer = (y == 0) | (y == DIMS[1] - 1)
    middle = (x == DIMS[0] // 2 - 1) | (x == DIMS[0] // 2)
    return jnp.where(z < DIMS[2] - 1, (x < DIMS[0] // 2) != (outer & middle), lax.rem(y, 2) == 0)


class Place:
    def __init__(self, dev, count):
        wrap = lambda i: lax.rem(i + 2 * count, count)
        self.dev, self.count, self.wrap = dev, count, wrap
        core = lax.rem(dev, 2)
        chip = dev // 2
        s = 2 * core - 1
        self.s = s
        self.ahead = wrap(dev + 2 * s)
        self.behind = wrap(dev - 2 * s)
        self.far = wrap(dev - 3 * s)
        self.sib = dev - s
        self.side = wrap(dev + s)
        before = lax.rem(chip + count // 2 - 1, count // 2)
        first = core == 0
        self.two = jnp.where(first, jnp.logical_not(upward(chip)), upward(before))
        other = jnp.where(first, upward(before), jnp.logical_not(upward(chip)))
        self.cross = jnp.where(self.two == other, core == 1, self.two)
        self.one = jnp.logical_not(self.two)
        self.pair = jnp.logical_not(self.cross)
        self.uses_sib = jnp.logical_or(self.one, self.pair)
        x, y, z = chip // (DIMS[1] * DIMS[2]), lax.rem(chip // DIMS[2], DIMS[1]), lax.rem(chip, DIMS[2])
        turn = jnp.where(first, z == DIMS[2] - 1, z == 0)
        across = dev + (DIMS[0] - 1 - 2 * x) * (2 * DIMS[1] * DIMS[2])
        self.relay = jnp.where(turn, wrap(dev - s * 2 * DIMS[2]), across)
        self.source = jnp.where(turn, wrap(dev + s * 2 * DIMS[2]), across)


def kernel(count, x_hbm, e_hbm, o_ref, raw, blk, rel, kst, bl, dacc, total, drecv, ebuf, sbuf, ymsg, yrecv, yacc,
           load_sem, sib_s, sib_r, f1_s, f1_r, f2_s, f2_r, g_s, g_r, rel_s, rel_r, e_s, e_r, y_s, y_r, d_s, d_r):
    tiles, width = raw.shape
    chunks = tiles // CR
    half = chunks // 2
    a = math.sqrt(2.0 * width) / width * math.log2(math.e)
    me = Place(lax.axis_index("dev"), count)
    sib = Place(me.sib, count)
    side = Place(me.side, count)

    loads = [pltpu.make_async_copy(x_hbm.at[pl.ds(c * CR, CR)], raw.at[pl.ds(c * CR, CR)], load_sem.at[c]) for c in range(chunks)]
    loads.append(pltpu.make_async_copy(e_hbm, ebuf.at[OWN], load_sem.at[chunks]))
    for load in loads:
        load.start()

    partners = [me.sib, me.side, me.ahead, me.behind, me.far]
    source = Place(me.source, count)
    onward = source.far
    partners += [me.relay, me.source, onward, Place(me.far, count).relay]
    barrier = pltpu.get_barrier_semaphore()
    for partner in partners:
        pl.semaphore_signal(barrier, inc=1, device_id=(partner,), device_id_type=MESH)

    def rows(c):
        return pl.ds(c * CR if isinstance(c, int) else pl.multiple_of(c * CR, CR), CR)

    def remote(src, dst, send, recv, to):
        return pltpu.make_async_remote_copy(src_ref=src, dst_ref=dst, send_sem=send, recv_sem=recv, device_id=(to,), device_id_type=MESH)

    def to_sib(c):
        return remote(blk.at[OWN, rows(c)], blk.at[SIB, rows(c)], sib_s.at[c], sib_r.at[c], me.sib)

    def to_ahead(c):
        return remote(blk.at[OWN, rows(c)], blk.at[F1, rows(c)], f1_s.at[c], f1_r.at[c], me.ahead)

    def to_far(c):
        return remote(blk.at[OWN, rows(c)], blk.at[F2, rows(c)], f2_s.at[c], f2_r.at[c], me.far)

    def to_relay(c):
        return remote(blk.at[OWN, rows(c)], rel.at[rows(c - half)], rel_s.at[c - half], rel_r.at[c - half], me.relay)

    def to_onward(c):
        return remote(rel.at[rows(c - half)], blk.at[F2, rows(c)], f2_s.at[c], f2_r.at[c], onward)

    def to_g(c):
        return remote(blk.at[F1, rows(c)], blk.at[G, rows(c)], g_s.at[c], g_r.at[c], me.sib)

    eye = lax.broadcasted_iota(jnp.int32, (128, 128), 0) == lax.broadcasted_iota(jnp.int32, (128, 128), 1)

    def laid(column):
        parts = []
        for start in range(0, column.shape[0], 128):
            wide = jnp.broadcast_to(column[start:start + 128], (128, 128))
            parts.append(jnp.sum(jnp.where(eye, wide, 0.0), axis=0, keepdims=True))
        return jnp.concatenate(parts, axis=1)

    def offsets(unit):
        values = unit.astype(F32)
        return (0.5 * a) * jnp.sum(values * values, axis=-1, keepdims=True)

    def normalize(c):
        values = raw[rows(c), :].astype(F32)
        mean = jnp.mean(values * values, axis=-1, keepdims=True)
        unit = (values * lax.rsqrt(mean + 1e-06)).astype(BF16)
        blk[OWN, rows(c), :] = unit
        bl[OWN, rows(c), :] = jnp.broadcast_to(offsets(unit), (CR, 128))

    def lay_offsets(slot):
        @pl.loop(0, chunks)
        def _(c):
            bl[slot, rows(c), :] = jnp.broadcast_to(offsets(blk[slot, rows(c), :]), (CR, 128))

    def tile(row_slot, col_slot, c, store, diagonal=False):
        unit = blk[col_slot, rows(c), :]
        inner = lax.dot_general(blk[row_slot], unit, (((1,), (1,)), ((), ())), preferred_element_type=F32)
        value = jnp.exp2(a * inner - jnp.concatenate([bl[row_slot]] * (CR // 128), axis=1) - laid(offsets(unit)))
        if diagonal:
            at = lax.broadcasted_iota(jnp.int32, value.shape, 1) + c * CR
            value = jnp.where(at == lax.broadcasted_iota(jnp.int32, value.shape, 0), 0.0, value)
        kst[store, :, rows(c)] = value.astype(BF16)
        dacc[col_slot, :, rows(c)] += jnp.sum(value, axis=0, keepdims=True)
        if not diagonal:
            dacc[row_slot] += laid(jnp.sum(value, axis=1, keepdims=True))

    dacc[...] = jnp.zeros_like(dacc)
    for c in range(chunks):
        loads[c].wait()
        normalize(c)
    pl.semaphore_wait(barrier, len(partners))
    for c in range(chunks):
        to_ahead(c).start()
        if c >= half:
            @pl.when(me.one)
            def _():
                to_relay(c).start()
        to_sib(c).start()

    loads[chunks].wait()

    def eig_to(slot, to):
        return remote(ebuf.at[OWN], ebuf.at[slot], e_s.at[slot], e_r.at[slot], to)

    eig_ahead, eig_far, eig_sib = eig_to(F1, me.ahead), eig_to(F2, me.far), eig_to(SIB, me.sib)
    eig_g = remote(ebuf.at[F1], ebuf.at[G], e_s.at[G], e_r.at[G], me.sib)
    @pl.when(sib.uses_sib)
    def _():
        eig_sib.start()

    @pl.loop(0, chunks)
    def _(c):
        tile(OWN, OWN, c, 0, diagonal=True)

    for c in range(chunks):
        to_sib(c).wait_recv()
    lay_offsets(SIB)

    @pl.when(me.pair)
    def _():
        @pl.loop(0, chunks)
        def _(c):
            tile(OWN, SIB, c, 3)

    @pl.loop(0, chunks)
    def _(c):
        to_ahead(c).wait_recv()

        @pl.when(sib.cross)
        def _():
            to_g(c).start()

        @pl.when(c == chunks - 2)
        def _():
            @pl.when(me.one)
            def _():
                @pl.loop(0, half)
                def _(i):
                    to_far(i).start()

            @pl.when(source.one)
            def _():
                @pl.loop(half, chunks)
                def _(i):
                    to_relay(i).wait_recv()
                    to_onward(i).start()

        tile(OWN, F1, c, 1)

        @pl.when(me.one)
        def _():
            tile(SIB, F1, c, 2)

    @pl.when(me.cross)
    def _():
        for c in range(chunks):
            to_g(c).wait_recv()
        lay_offsets(G)

        @pl.loop(0, chunks)
        def _(c):
            tile(G, F1, c, 3)

    owners = {OWN: me, F1: Place(me.behind, count), G: side, F2: Place(me.far, count), SIB: sib}
    held = {OWN: None, F1: None, G: me.cross, F2: me.two, SIB: me.uses_sib}

    def member(owner, kind):
        if kind == OWN:
            return owner.dev, None
        if kind == F1:
            return owner.ahead, None
        if kind == G:
            return owner.side, Place(owner.side, count).cross
        if kind == F2:
            return owner.far, owner.one
        return owner.sib, Place(owner.sib, count).uses_sib

    def given(conditions, action):
        known = [c for c in conditions if c is not None]
        if known:
            pl.when(functools.reduce(jnp.logical_and, known))(action)
        else:
            action()

    def part(slot, kind):
        dev, exists = member(owners[slot], kind)
        out = lambda: remote(dacc.at[slot], drecv.at[kind, slot], d_s.at[slot, kind], d_r.at[kind, slot], dev)
        back = lambda: remote(dacc.at[kind], drecv.at[slot, kind], d_s.at[kind, slot], d_r.at[slot, kind], dev)
        return out, back, (held[slot], exists)

    kinds = (OWN, F1, G, F2, SIB)

    def send_parts(slot):
        for kind in kinds:
            if kind != slot:
                out, _, when = part(slot, kind)
                given(when, lambda: out().start())

    @pl.when(me.two)
    def _():
        eig_ahead.start()

    send_parts(F1)
    send_parts(G)
    send_parts(SIB)

    @pl.when(me.two)
    def _():
        @pl.loop(0, chunks)
        def _(i):
            c = i // 2 + lax.rem(i, 2) * half
            to_far(c).wait_recv()
            tile(OWN, F2, c, 2)

    send_parts(OWN)
    send_parts(F2)

    @pl.when(me.one)
    def _():
        for c in range(half):
            to_far(c).wait_send()
        eig_far.start()
        eig_ahead.start()


    def scale(slot):
        for kind in kinds:
            if kind != slot:
                _, back, when = part(slot, kind)

                def add(back=back, kind=kind):
                    back().wait_recv()
                    total[slot] += drecv[slot, kind]

                given(when, add)
        inverse = lax.rsqrt(total[slot])
        sbuf[slot] = (ebuf[slot].astype(F32) * inverse).astype(BF16)

    def by_columns(slot, store):
        return jnp.dot(sbuf[slot], kst[store], preferred_element_type=F32)

    def by_rows(slot, store):
        return lax.dot_general(sbuf[slot], kst[store], (((1,), (1,)), ((), ())), preferred_element_type=F32)

    def returns(slot):
        out = remote(ymsg.at[slot], yrecv.at[slot], y_s.at[slot], y_r.at[slot], owners[slot].dev)
        return out, held[slot], member(me, slot)[1]

    def give(slot, value):
        ymsg[slot] = value.astype(BF16)
        returns(slot)[0].start()

    total[...] = dacc[...]
    scale(OWN)

    @pl.when(me.two)
    def _():
        give(F2, by_columns(OWN, 2))

    yacc[F1] = by_columns(OWN, 1)
    eig_ahead.wait_recv()

    @pl.when(sib.cross)
    def _():
        eig_g.start()

    @pl.when(me.uses_sib)
    def _():
        eig_sib.wait_recv()
        scale(SIB)

        @pl.when(me.one)
        def _():
            yacc[F1] += by_columns(SIB, 2)

    @pl.when(me.cross)
    def _():
        eig_g.wait_recv()
        scale(G)
        yacc[F1] += by_columns(G, 3)

    give(F1, yacc[F1])
    scale(F1)

    @pl.when(me.cross)
    def _():
        give(G, by_rows(F1, 3))

    @pl.when(me.uses_sib)
    def _():
        yacc[SIB] = jnp.zeros_like(yacc[SIB])

        @pl.when(me.one)
        def _():
            yacc[SIB] += by_rows(F1, 2)

        @pl.when(me.pair)
        def _():
            yacc[SIB] += by_columns(OWN, 3)

        give(SIB, yacc[SIB])

    yacc[OWN] = by_columns(OWN, 0)
    yacc[OWN] += by_rows(F1, 1)

    @pl.when(me.two)
    def _():
        eig_far.wait_recv()
        scale(F2)
        yacc[OWN] += by_rows(F2, 2)

    @pl.when(me.pair)
    def _():
        yacc[OWN] += by_rows(SIB, 3)

    for slot in (SIB, F2, G, F1):
        copy, _, receives = returns(slot)

        def gather(copy=copy, slot=slot):
            copy.wait_recv()
            yacc[OWN] += yrecv[slot].astype(F32)

        given((receives,), gather)
    inverse = lax.rsqrt(total[OWN])
    factor = 0.25 * math.sqrt((2 * ROUNDS + 1) * tiles)
    o_ref[...] = (factor * inverse) * yacc[OWN]

    for c in range(chunks):
        to_ahead(c).wait_send()
        to_sib(c).wait_send()

    @pl.when(sib.cross)
    def _():
        for c in range(chunks):
            to_g(c).wait_send()

    @pl.when(me.one)
    def _():
        for c in range(half, chunks):
            to_relay(c).wait_send()

    @pl.when(source.one)
    def _():
        for c in range(half, chunks):
            to_onward(c).wait_send()

    eig_ahead.wait_send()
    given((sib.uses_sib,), eig_sib.wait_send)
    given((me.one,), eig_far.wait_send)
    given((sib.cross,), eig_g.wait_send)
    for slot in kinds:
        for kind in kinds:
            if kind != slot:
                out, _, when = part(slot, kind)
                given(when, lambda: out().wait_send())
        if slot != OWN:
            copy, sends, _ = returns(slot)
            given((sends,), copy.wait_send)


def shards(count, features, eigvecs):
    tiles, width = features.shape
    rank = eigvecs.shape[1]
    chunks = tiles // CR
    dma = lambda n: pltpu.SemaphoreType.DMA((n,))
    out = pl.pallas_call(
        functools.partial(kernel, count),
        out_shape=jax.ShapeDtypeStruct((rank, tiles), F32),
        in_specs=[pl.BlockSpec(memory_space=pl.ANY)] * 2,
        out_specs=pl.BlockSpec(memory_space=pltpu.VMEM),
        scratch_shapes=[
            pltpu.VMEM((tiles, width), BF16),
            pltpu.VMEM((5, tiles, width), BF16),
            pltpu.VMEM((tiles // 2, width), BF16),
            pltpu.VMEM((4, tiles, tiles), BF16),
            pltpu.VMEM((5, tiles, 128), F32),
            pltpu.VMEM((5, 1, tiles), F32),
            pltpu.VMEM((5, 1, tiles), F32),
            pltpu.VMEM((5, 5, 1, tiles), F32),
            pltpu.VMEM((5, rank, tiles), BF16),
            pltpu.VMEM((5, rank, tiles), BF16),
            pltpu.VMEM((5, rank, tiles), BF16),
            pltpu.VMEM((5, rank, tiles), BF16),
            pltpu.VMEM((5, rank, tiles), F32),
            dma(chunks + 1),
        ] + [dma(chunks)] * 10 + [dma(5)] * 4 + [pltpu.SemaphoreType.DMA((5, 5))] * 2,
        compiler_params=pltpu.CompilerParams(
            collective_id=0, has_side_effects=True, vmem_limit_bytes=56 * 2**20
        ),
        name="cluster",
    )(features, eigvecs.T)
    return out.T


def solution(mesh):
    return jax.shard_map(
        functools.partial(shards, mesh.shape["dev"]),
        mesh=mesh,
        in_specs=(P("dev", None), P("dev", None)),
        out_specs=P("dev", None),
        check_vma=False,
    )
```

```python
import functools
import math

import jax
import jax.numpy as jnp
from jax import lax
from jax.experimental import pallas as pl
from jax.experimental.pallas import tpu as pltpu
from jax.sharding import PartitionSpec as P

ROUNDS = 3
MESH = pl.DeviceIdType.MESH
OWN, SIB, F1, F2, G = range(5)
CR = 256
CROSSING = 2
DIMS = (4, 4, 8)
F32, BF16 = jnp.float32, jnp.bfloat16


def upward(chip):
    x, y, z = chip // (DIMS[1] * DIMS[2]), lax.rem(chip // DIMS[2], DIMS[1]), lax.rem(chip, DIMS[2])
    outer = (y == 0) | (y == DIMS[1] - 1)
    middle = (x == DIMS[0] // 2 - 1) | (x == DIMS[0] // 2)
    return jnp.where(z < DIMS[2] - 1, (x < DIMS[0] // 2) != (outer & middle), lax.rem(y, 2) == 0)


class Place:
    def __init__(self, dev, count):
        wrap = lambda i: lax.rem(i + 2 * count, count)
        self.dev, self.count, self.wrap = dev, count, wrap
        core = lax.rem(dev, 2)
        chip = dev // 2
        s = 2 * core - 1
        self.s = s
        self.ahead = wrap(dev + 2 * s)
        self.behind = wrap(dev - 2 * s)
        self.far = wrap(dev - 3 * s)
        self.sib = dev - s
        self.side = wrap(dev + s)
        before = lax.rem(chip + count // 2 - 1, count // 2)
        first = core == 0
        self.two = jnp.where(first, jnp.logical_not(upward(chip)), upward(before))
        other = jnp.where(first, upward(before), jnp.logical_not(upward(chip)))
        self.cross = jnp.where(self.two == other, core == 1, self.two)
        self.one = jnp.logical_not(self.two)
        self.pair = jnp.logical_not(self.cross)
        self.uses_sib = jnp.logical_or(self.one, self.pair)
        x, y, z = chip // (DIMS[1] * DIMS[2]), lax.rem(chip // DIMS[2], DIMS[1]), lax.rem(chip, DIMS[2])
        turn = jnp.where(first, z == DIMS[2] - 1, z == 0)
        across = dev + (DIMS[0] - 1 - 2 * x) * (2 * DIMS[1] * DIMS[2])
        column = lambda step: dev + (lax.rem(y + DIMS[1] + step, DIMS[1]) - y) * (2 * DIMS[2])
        self.relay = jnp.where(turn, column(-s), across)
        self.source = jnp.where(turn, column(s), across)
        self.direct = jnp.where(jnp.logical_not(first) & (z == 0) & (y == 0), CROSSING, 2)


def kernel(count, x_hbm, e_hbm, o_ref, raw, blk, rel, kst, bl, dacc, total, drecv, ebuf, sbuf, ymsg, yrecv, yacc,
           load_sem, sib_s, sib_r, f1_s, f1_r, f2_s, f2_r, g_s, g_r, rel_s, rel_r, e_s, e_r, y_s, y_r, d_s, d_r):
    tiles, width = raw.shape
    chunks = tiles // CR
    a = math.sqrt(2.0 * width) / width * math.log2(math.e)
    me = Place(lax.axis_index("dev"), count)
    sib = Place(me.sib, count)
    side = Place(me.side, count)

    loads = [pltpu.make_async_copy(x_hbm.at[pl.ds(c * CR, CR)], raw.at[pl.ds(c * CR, CR)], load_sem.at[c]) for c in range(chunks)]
    loads.append(pltpu.make_async_copy(e_hbm, ebuf.at[OWN], load_sem.at[chunks]))
    for load in loads:
        load.start()

    partners = [me.sib, me.side, me.ahead, me.behind, me.far]
    source = Place(me.source, count)
    onward = source.far
    far = Place(me.far, count)
    partners += [me.relay, me.source, onward, far.relay]
    barrier = pltpu.get_barrier_semaphore()
    for partner in partners:
        pl.semaphore_signal(barrier, inc=1, device_id=(partner,), device_id_type=MESH)

    def rows(c):
        return pl.ds(c * CR if isinstance(c, int) else pl.multiple_of(c * CR, CR), CR)

    def remote(src, dst, send, recv, to):
        return pltpu.make_async_remote_copy(src_ref=src, dst_ref=dst, send_sem=send, recv_sem=recv, device_id=(to,), device_id_type=MESH)

    def to_sib(c):
        return remote(blk.at[OWN, rows(c)], blk.at[SIB, rows(c)], sib_s.at[c], sib_r.at[c], me.sib)

    def to_ahead(c):
        return remote(blk.at[OWN, rows(c)], blk.at[F1, rows(c)], f1_s.at[c], f1_r.at[c], me.ahead)

    def to_far(c):
        return remote(blk.at[OWN, rows(c)], blk.at[F2, rows(c)], f2_s.at[c], f2_r.at[c], me.far)

    def to_relay(c):
        return remote(blk.at[OWN, rows(c)], rel.at[rows(c)], rel_s.at[c], rel_r.at[c], me.relay)

    def to_onward(c):
        return remote(rel.at[rows(c)], blk.at[F2, rows(c)], f2_s.at[c], f2_r.at[c], onward)

    def to_g(c):
        return remote(blk.at[F1, rows(c)], blk.at[G, rows(c)], g_s.at[c], g_r.at[c], me.sib)

    eye = lax.broadcasted_iota(jnp.int32, (128, 128), 0) == lax.broadcasted_iota(jnp.int32, (128, 128), 1)

    def laid(column):
        parts = []
        for start in range(0, column.shape[0], 128):
            wide = jnp.broadcast_to(column[start:start + 128], (128, 128))
            parts.append(jnp.sum(jnp.where(eye, wide, 0.0), axis=0, keepdims=True))
        return jnp.concatenate(parts, axis=1)

    def offsets(unit):
        values = unit.astype(F32)
        return (0.5 * a) * jnp.sum(values * values, axis=-1, keepdims=True)

    def normalize(c):
        values = raw[rows(c), :].astype(F32)
        mean = jnp.mean(values * values, axis=-1, keepdims=True)
        unit = (values * lax.rsqrt(mean + 1e-06)).astype(BF16)
        blk[OWN, rows(c), :] = unit
        bl[OWN, rows(c), :] = jnp.broadcast_to(offsets(unit), (CR, 128))

    def lay_offsets(slot):
        @pl.loop(0, chunks)
        def _(c):
            bl[slot, rows(c), :] = jnp.broadcast_to(offsets(blk[slot, rows(c), :]), (CR, 128))

    def tile(row_slot, col_slot, c, store, diagonal=False):
        unit = blk[col_slot, rows(c), :]
        inner = lax.dot_general(blk[row_slot], unit, (((1,), (1,)), ((), ())), preferred_element_type=F32)
        value = jnp.exp2(a * inner - jnp.concatenate([bl[row_slot]] * (CR // 128), axis=1) - laid(offsets(unit)))
        if diagonal:
            at = lax.broadcasted_iota(jnp.int32, value.shape, 1) + c * CR
            value = jnp.where(at == lax.broadcasted_iota(jnp.int32, value.shape, 0), 0.0, value)
        kst[store, :, rows(c)] = value.astype(BF16)
        dacc[col_slot, :, rows(c)] += jnp.sum(value, axis=0, keepdims=True)
        if not diagonal:
            dacc[row_slot] += laid(jnp.sum(value, axis=1, keepdims=True))

    dacc[...] = jnp.zeros_like(dacc)
    for c in range(chunks):
        loads[c].wait()
        normalize(c)
    pl.semaphore_wait(barrier, len(partners))
    for c in range(chunks):
        to_ahead(c).start()
        if c > 0:
            @pl.when(me.one & (c >= me.direct))
            def _():
                to_relay(c).start()
        to_sib(c).start()

    loads[chunks].wait()

    def eig_to(slot, to):
        return remote(ebuf.at[OWN], ebuf.at[slot], e_s.at[slot], e_r.at[slot], to)

    eig_ahead, eig_far, eig_sib = eig_to(F1, me.ahead), eig_to(F2, me.far), eig_to(SIB, me.sib)
    eig_g = remote(ebuf.at[F1], ebuf.at[G], e_s.at[G], e_r.at[G], me.sib)
    @pl.when(sib.uses_sib)
    def _():
        eig_sib.start()

    @pl.loop(0, chunks)
    def _(c):
        tile(OWN, OWN, c, 0, diagonal=True)

    for c in range(chunks):
        to_sib(c).wait_recv()
    lay_offsets(SIB)

    @pl.when(me.pair)
    def _():
        @pl.loop(0, chunks)
        def _(c):
            tile(OWN, SIB, c, 3)

    @pl.loop(0, chunks)
    def _(c):
        to_ahead(c).wait_recv()

        @pl.when(sib.cross)
        def _():
            to_g(c).start()

        @pl.when((c == chunks - 2) & me.one)
        def _():
            @pl.loop(0, me.direct)
            def _(i):
                to_far(i).start()

        @pl.when((c == chunks - 2) & source.one)
        def _():
            @pl.loop(source.direct, chunks)
            def _(i):
                to_relay(i).wait_recv()
                to_onward(i).start()

        tile(OWN, F1, c, 1)

        @pl.when(me.one)
        def _():
            tile(SIB, F1, c, 2)

    @pl.when(me.cross)
    def _():
        for c in range(chunks):
            to_g(c).wait_recv()
        lay_offsets(G)

        @pl.loop(0, chunks)
        def _(c):
            tile(G, F1, c, 3)

    owners = {OWN: me, F1: Place(me.behind, count), G: side, F2: far, SIB: sib}
    held = {OWN: None, F1: None, G: me.cross, F2: me.two, SIB: me.uses_sib}

    def member(owner, kind):
        if kind == OWN:
            return owner.dev, None
        if kind == F1:
            return owner.ahead, None
        if kind == G:
            return owner.side, Place(owner.side, count).cross
        if kind == F2:
            return owner.far, owner.one
        return owner.sib, Place(owner.sib, count).uses_sib

    def given(conditions, action):
        known = [c for c in conditions if c is not None]
        if known:
            pl.when(functools.reduce(jnp.logical_and, known))(action)
        else:
            action()

    def part(slot, kind):
        dev, exists = member(owners[slot], kind)
        out = lambda: remote(dacc.at[slot], drecv.at[kind, slot], d_s.at[slot, kind], d_r.at[kind, slot], dev)
        back = lambda: remote(dacc.at[kind], drecv.at[slot, kind], d_s.at[kind, slot], d_r.at[slot, kind], dev)
        return out, back, (held[slot], exists)

    kinds = (OWN, F1, G, F2, SIB)

    def send_parts(slot):
        for kind in kinds:
            if kind != slot:
                out, _, when = part(slot, kind)
                given(when, lambda: out().start())

    @pl.when(me.two)
    def _():
        eig_ahead.start()

    send_parts(F1)
    send_parts(G)
    send_parts(SIB)

    @pl.when(me.two)
    def _():
        @pl.loop(0, chunks)
        def _(i):
            c = jnp.where(i == chunks - 1, i, lax.rem(jnp.where(far.direct == 1, i + 1, 2 * i), 3))
            to_far(c).wait_recv()
            tile(OWN, F2, c, 2)

    send_parts(OWN)
    send_parts(F2)

    @pl.when(me.one)
    def _():
        @pl.loop(0, me.direct)
        def _(c):
            to_far(c).wait_send()

        eig_far.start()
        eig_ahead.start()


    def scale(slot):
        for kind in kinds:
            if kind != slot:
                _, back, when = part(slot, kind)

                def add(back=back, kind=kind):
                    back().wait_recv()
                    total[slot] += drecv[slot, kind]

                given(when, add)
        inverse = lax.rsqrt(total[slot])
        sbuf[slot] = (ebuf[slot].astype(F32) * inverse).astype(BF16)

    def by_columns(slot, store):
        return jnp.dot(sbuf[slot], kst[store], preferred_element_type=F32)

    def by_rows(slot, store):
        return lax.dot_general(sbuf[slot], kst[store], (((1,), (1,)), ((), ())), preferred_element_type=F32)

    def returns(slot):
        out = remote(ymsg.at[slot], yrecv.at[slot], y_s.at[slot], y_r.at[slot], owners[slot].dev)
        return out, held[slot], member(me, slot)[1]

    def give(slot, value):
        ymsg[slot] = value.astype(BF16)
        returns(slot)[0].start()

    total[...] = dacc[...]
    scale(OWN)

    @pl.when(me.two)
    def _():
        give(F2, by_columns(OWN, 2))

    yacc[F1] = by_columns(OWN, 1)
    eig_ahead.wait_recv()

    @pl.when(sib.cross)
    def _():
        eig_g.start()

    @pl.when(me.uses_sib)
    def _():
        eig_sib.wait_recv()
        scale(SIB)

        @pl.when(me.one)
        def _():
            yacc[F1] += by_columns(SIB, 2)

    @pl.when(me.cross)
    def _():
        eig_g.wait_recv()
        scale(G)
        yacc[F1] += by_columns(G, 3)

    give(F1, yacc[F1])
    scale(F1)

    @pl.when(me.cross)
    def _():
        give(G, by_rows(F1, 3))

    @pl.when(me.uses_sib)
    def _():
        yacc[SIB] = jnp.zeros_like(yacc[SIB])

        @pl.when(me.one)
        def _():
            yacc[SIB] += by_rows(F1, 2)

        @pl.when(me.pair)
        def _():
            yacc[SIB] += by_columns(OWN, 3)

        give(SIB, yacc[SIB])

    yacc[OWN] = by_columns(OWN, 0)
    yacc[OWN] += by_rows(F1, 1)

    @pl.when(me.two)
    def _():
        eig_far.wait_recv()
        scale(F2)
        yacc[OWN] += by_rows(F2, 2)

    @pl.when(me.pair)
    def _():
        yacc[OWN] += by_rows(SIB, 3)

    for slot in (SIB, F2, G, F1):
        copy, _, receives = returns(slot)

        def gather(copy=copy, slot=slot):
            copy.wait_recv()
            yacc[OWN] += yrecv[slot].astype(F32)

        given((receives,), gather)
    inverse = lax.rsqrt(total[OWN])
    factor = 0.25 * math.sqrt((2 * ROUNDS + 1) * tiles)
    o_ref[...] = (factor * inverse) * yacc[OWN]

    for c in range(chunks):
        to_ahead(c).wait_send()
        to_sib(c).wait_send()

    @pl.when(sib.cross)
    def _():
        for c in range(chunks):
            to_g(c).wait_send()

    @pl.when(me.one)
    def _():
        @pl.loop(me.direct, chunks)
        def _(c):
            to_relay(c).wait_send()

    @pl.when(source.one)
    def _():
        @pl.loop(source.direct, chunks)
        def _(c):
            to_onward(c).wait_send()

    eig_ahead.wait_send()
    given((sib.uses_sib,), eig_sib.wait_send)
    given((me.one,), eig_far.wait_send)
    given((sib.cross,), eig_g.wait_send)
    for slot in kinds:
        for kind in kinds:
            if kind != slot:
                out, _, when = part(slot, kind)
                given(when, lambda: out().wait_send())
        if slot != OWN:
            copy, sends, _ = returns(slot)
            given((sends,), copy.wait_send)


def shards(count, features, eigvecs):
    tiles, width = features.shape
    rank = eigvecs.shape[1]
    chunks = tiles // CR
    dma = lambda n: pltpu.SemaphoreType.DMA((n,))
    out = pl.pallas_call(
        functools.partial(kernel, count),
        out_shape=jax.ShapeDtypeStruct((rank, tiles), F32),
        in_specs=[pl.BlockSpec(memory_space=pl.ANY)] * 2,
        out_specs=pl.BlockSpec(memory_space=pltpu.VMEM),
        scratch_shapes=[
            pltpu.VMEM((tiles, width), BF16),
            pltpu.VMEM((5, tiles, width), BF16),
            pltpu.VMEM((tiles, width), BF16),
            pltpu.VMEM((4, tiles, tiles), BF16),
            pltpu.VMEM((5, tiles, 128), F32),
            pltpu.VMEM((5, 1, tiles), F32),
            pltpu.VMEM((5, 1, tiles), F32),
            pltpu.VMEM((5, 5, 1, tiles), F32),
            pltpu.VMEM((5, rank, tiles), BF16),
            pltpu.VMEM((5, rank, tiles), BF16),
            pltpu.VMEM((5, rank, tiles), BF16),
            pltpu.VMEM((5, rank, tiles), BF16),
            pltpu.VMEM((5, rank, tiles), F32),
            dma(chunks + 1),
        ] + [dma(chunks)] * 10 + [dma(5)] * 4 + [pltpu.SemaphoreType.DMA((5, 5))] * 2,
        compiler_params=pltpu.CompilerParams(
            collective_id=0, has_side_effects=True, vmem_limit_bytes=56 * 2**20
        ),
        name="cluster",
    )(features, eigvecs.T)
    return out.T


def solution(mesh):
    return jax.shard_map(
        functools.partial(shards, mesh.shape["dev"]),
        mesh=mesh,
        in_specs=(P("dev", None), P("dev", None)),
        out_specs=P("dev", None),
        check_vma=False,
    )
```
